1024 devices in a mesh: section: 16 (over x, y), expert: 64 (over z, core).
Axes of the slice: x: 4, y: 4, z: 32, core: 2. Of those that a mesh axis runs over, the one named last changes fastest.
Arguments:
- tokens: bfloat16 [16, 2048, 2048], P('section', 'expert'), may hold values from -6 to 6
- norm_gain: float32 [2048], replicated, may hold values from 0.1 to 1.9
- route_ids: int32 [16, 2048, 8], P('section', 'expert'), may hold values from 0 to 63, all different within a row; in each aligned block of 32 rows (0 to 31, 32 to 63, ..., all dimensions but the last counted through in order) at most 6 rows name the same one
- route_weight: float32 [16, 2048, 8], P('section', 'expert'), may hold values from 0.05 to 1
- gate_up: bfloat16 [64, 2048, 1536], P('expert'), may hold values from -0.125 to 0.125
- down: bfloat16 [64, 768, 2048], P('expert'), may hold values from -0.21875 to 0.21875
Outputs:
- next_rows: bfloat16 [16, 2048, 2048], P('section', 'expert')
The draws below stay inside these ranges and needn't reach their ends.
Inputs may be any that keep to these rules, and one draw needn't show every extreme that they name: `route_ids`: each row names 8 different experts. In each aligned block of 32 rows of a section (the rows of one device), no expert is named by more than 6 entries.
All inputs are finite; a program needn't handle non-finite values.
Results may differ from the reference program's by a relative error of at most 0.0039.
Values may be sent and summed in bfloat16 or wider, within the bound.
No kernel may reach another device: no remote copies, remote signals or barrier semaphores. Data moves between devices by JAX's collectives and lax.ppermute only.
A program may use at most 32 MiB of HBM per device.

```python
import math
import jax
import jax.numpy as jnp
import numpy as np
from jax import lax

D = 2048
HID = 768
EXPERTS = 64
TOPK = 8
CAP = 6
TOK_DEV = 32
TOKENS = 2048
N_SECTION = 16
N_EXPERT = 64


def steps_of(key, dims, split, least, top_value):
    loudness, own = 1.0, jax.random.fold_in(key, 6)
    for axis_at, shards_of in split:
        draws = jnp.exp(jax.random.uniform(jax.random.fold_in(own, axis_at), (shards_of,), jnp.float32, least / len(split), top_value / len(split)))
        loudness = loudness * jnp.repeat(draws, dims[axis_at] // shards_of).reshape([-1 if axis == axis_at else 1 for axis in range(len(dims))])
    return loudness


def deal_out(rng, own, number, rows, number_of, top, bound, slope):
    sequence = jax.random.permutation(rng, number_of)
    heavy_load, ordinary = load_shares(number_of, rows * top, bound, slope, True), load_shares(number_of, rows * top, bound, slope, False)
    places = jnp.arange(number_of)

    def named(lengths, rotation):
        used = int((lengths > 0).sum())
        fixed = max(1, used // 4)
        passed = fixed + (places - fixed + rotation * (used - fixed)) % max(1, number_of - fixed)
        return jnp.zeros((number_of,), jnp.int32).at[sequence[jnp.where(places < fixed, places, passed)]].set(jnp.asarray(lengths, jnp.int32))

    lengths = jnp.where(number % 4 == 0, named(heavy_load, number // 4), named(ordinary, number - number // 4 - 1))
    mixed = jax.random.permutation(jax.random.fold_in(own, 3), number_of)
    donor, taker = mixed[0:number_of // 2 * 2:2], mixed[1:number_of // 2 * 2:2]
    margin = jnp.minimum(lengths[donor] - 1, bound - lengths[taker]) // 2
    margin = jnp.where((donor == sequence[0]) | (taker == sequence[0]) | (lengths[taker] == 0), 0, jnp.maximum(margin, 0))
    passed = jax.random.randint(jax.random.fold_in(own, 4), (number_of // 2,), 0, 1 << 20) % (margin + 1)
    lengths = lengths.at[donor].add(-passed).at[taker].add(passed)
    members = jnp.searchsorted(jnp.cumsum(lengths), jnp.arange(rows * top), side="right").astype(jnp.int32)
    table = members.reshape(top, rows).T
    table = table[jax.random.permutation(jax.random.fold_in(own, 1), rows)]
    rotation = jax.random.randint(jax.random.fold_in(own, 2), (rows, 1), 0, top)
    return jnp.take_along_axis(table, (jnp.arange(top)[None, :] + rotation) % top, axis=1)


def load_shares(count, total, bound, lean, full):
    weights = [(1 << 20) // math.isqrt(standing ** lean) + 1 for standing in range(1, count + 1)]
    largest = bound if full else min(bound, max(-(-total // count), total * weights[0] // sum(weights)))
    least = 1 if total - largest >= count - 1 else 0
    given, surplus = [largest] + [least] * (count - 1), total - largest - least * (count - 1)
    while surplus > 0:
        movable = [i for i in range(1, count) if given[i] < largest] or [i for i in range(1, count) if given[i] < bound]
        whole, left = sum([weights[i] for i in movable]), surplus
        for i in movable:
            more = min(bound - given[i], max(1, left * weights[i] // whole), surplus)
            given[i] = given[i] + more
            surplus = surplus - more
    return np.array(given)


def scatter_about(stream_key, shape, scale, limit, split=(), kind=jnp.bfloat16):
    result = scale * jax.random.normal(stream_key, shape, jnp.float32)
    if split:
        result = result * steps_of(stream_key, shape, split, -0.22, 0.18)
    return jnp.clip(result, -limit, limit).astype(kind)


def setup_inputs(seed: int = 0) -> dict:
    splits = jax.random.split(jax.random.key(seed), 7)
    tokens = scatter_about(splits[0], (N_SECTION, TOKENS, D), 1.0, 6.0, ((0, 16), (1, 64)))
    norm_gain = jnp.clip(1.0 + 0.18 * jax.random.normal(splits[1], (D,), jnp.float32), 0.1, 1.9)
    route_ids_keys = jax.random.split(jax.random.fold_in(splits[2], 1), N_SECTION * TOKENS // TOK_DEV)
    route_ids_turns = jax.random.permutation(jax.random.fold_in(splits[2], 3), N_SECTION * TOKENS // TOK_DEV)
    route_ids = jax.vmap(lambda own, number: deal_out(jax.random.fold_in(splits[2], 2), own, number, TOK_DEV, EXPERTS, TOPK, CAP, 2))(route_ids_keys, route_ids_turns).reshape((N_SECTION, TOKENS, TOPK))
    route_weight = jnp.clip(jnp.exp(math.log(1.0) - 2.9957323 * jax.random.uniform(splits[3], (N_SECTION, TOKENS, TOPK), jnp.float32) ** steps_of(splits[3], (N_SECTION, TOKENS, TOPK), ((0, 16), (1, 64)), -0.2, 0.2)), 0.05, 1.0)
    gate_up = scatter_about(splits[4], (EXPERTS, D, 2 * HID), D ** -0.5, 0.125, ((0, 64),))
    down = scatter_about(splits[5], (EXPERTS, HID, D), HID ** -0.5, 0.21875, ((0, 64),))
    return dict(tokens=tokens, norm_gain=norm_gain, route_ids=route_ids, route_weight=route_weight, gate_up=gate_up, down=down)


def section_layer(rows, ids, weights, gain, wide_gu, wide_down):
    hp = lax.Precision.HIGHEST
    slots = EXPERTS * CAP
    values = rows.astype(jnp.float32)
    scale = lax.rsqrt(lax.optimization_barrier(jnp.mean(values * values, axis=1, keepdims=True)) + 1e-06)
    normed = (values * scale * gain[None, :]).astype(jnp.bfloat16)
    share = weights / lax.optimization_barrier(jnp.sum(weights, axis=1, keepdims=True))
    flat = ids.reshape(N_EXPERT, TOK_DEV * TOPK)
    onehot = (flat[:, :, None] == jnp.arange(EXPERTS, dtype=jnp.int32)[None, None, :]).astype(jnp.int32)
    rank = lax.optimization_barrier(jnp.sum((jnp.cumsum(onehot, axis=1) - onehot) * onehot, axis=2))
    slot = flat * CAP + rank
    select = (slot[:, :, None] == jnp.arange(slots, dtype=jnp.int32)[None, None, :]).astype(jnp.float32)
    select = select.reshape(N_EXPERT, TOK_DEV, TOPK, slots)
    place = lax.optimization_barrier(jnp.sum(select, axis=2))
    weighted = lax.optimization_barrier(jnp.sum(select * share.reshape(N_EXPERT, TOK_DEV, TOPK)[:, :, :, None], axis=2))
    blocks = normed.reshape(N_EXPERT, TOK_DEV, D).astype(jnp.float32)
    sent = jnp.einsum('bts,btd->bsd', place, blocks, precision=hp).astype(jnp.bfloat16)
    sent = sent.reshape(N_EXPERT, EXPERTS, CAP, D).transpose(1, 0, 2, 3)
    gated = jnp.einsum('ebcd,edf->ebcf', sent.astype(jnp.float32), wide_gu, precision=hp)
    hidden = (jax.nn.silu(gated[..., :HID]) * gated[..., HID:]).astype(jnp.bfloat16)
    answer = jnp.einsum('ebcf,efd->ebcd', hidden.astype(jnp.float32), wide_down, precision=hp).astype(jnp.bfloat16)
    answer = answer.transpose(1, 0, 2, 3).reshape(N_EXPERT, slots, D)
    branch = jnp.einsum('bts,bsd->btd', weighted, answer.astype(jnp.float32), precision=hp)
    return (values + branch.reshape(TOKENS, D)).astype(jnp.bfloat16)

def reference(tokens, norm_gain, route_ids, route_weight, gate_up, down):
    wide_gu = gate_up.astype(jnp.float32)
    wide_down = down.astype(jnp.float32)

    def one_section(packed):
        rows, ids, weights = packed
        return section_layer(rows, ids, weights, norm_gain, wide_gu, wide_down)
    outputs = lax.map(one_section, (tokens, route_ids, route_weight))
    return jnp.roll(outputs, 1, axis=0)
```

```python
import jax
import jax.numpy as jnp
from jax import lax
from jax.experimental import pallas as pl
from jax.experimental.pallas import tpu as pltpu
from jax.sharding import PartitionSpec as P

CAP = 6
ROWS = 32
INFO = 128
FAR = 4
BLOCKS = 8
SEG = BLOCKS * CAP
SLOTS = 8 * SEG
TILES = 3
VMEM = 56 * 2**20


def send(value, up, down, other=False, onward=0):
    count = lax.axis_size("expert")

    def place(i):
        chip, core = i // 2, i % 2
        if other:
            core = 1 - core
        return ((chip + (up if i % 2 == 0 else down)) * 2) % count + core

    if not onward:
        return lax.ppermute(value, "expert", [(i, place(i)) for i in range(count)])
    sections = lax.axis_size("section")
    pairs = [
        (s * count + i, (s + onward) % sections * count + place(i))
        for s in range(sections)
        for i in range(count)
    ]
    return lax.ppermute(value, ("section", "expert"), pairs)


def dispatch_kernel(expert_ref, *refs):
    blocks = refs[:BLOCKS]
    here, up1, down1, up2, down2, hi_ref, lo_ref = refs[BLOCKS:]
    width = here.shape[1]
    rows = BLOCKS * ROWS
    info = jnp.concatenate([b[:, width:] for b in blocks], axis=0).astype(jnp.float32)
    expert = expert_ref[0:1, :]
    member = jnp.zeros((rows, SLOTS), jnp.float32)
    hi = jnp.zeros((rows, SLOTS), jnp.float32)
    lo = jnp.zeros((rows, SLOTS), jnp.float32)
    for k in range(8):
        same = info[:, k : k + 1] == expert
        member = jnp.where(same, 1.0, member)
        hi = jnp.where(same, info[:, 8 + k : 9 + k], hi)
        lo = jnp.where(same, info[:, 16 + k : 17 + k], lo)
    r = lax.broadcasted_iota(jnp.int32, (rows, rows), 0)
    c = lax.broadcasted_iota(jnp.int32, (rows, rows), 1)
    before = jnp.where((c < r) & (c // ROWS == r // ROWS), 1.0, 0.0).astype(jnp.bfloat16)
    rank = jnp.dot(before, member.astype(jnp.bfloat16), preferred_element_type=jnp.float32)
    row_block = lax.broadcasted_iota(jnp.int32, (rows, SLOTS), 0) // ROWS
    q = lax.broadcasted_iota(jnp.int32, (rows, SLOTS), 1) % SEG
    taken = (member > 0.5) & (rank == (q % CAP).astype(jnp.float32)) & (q // CAP == row_block)
    hi_ref[...] = jnp.where(taken, hi, 0.0).astype(jnp.bfloat16)
    lo_ref[...] = jnp.where(taken, lo, 0.0).astype(jnp.bfloat16)
    pick = jnp.where(taken, 1.0, 0.0).astype(jnp.bfloat16)
    step = min(512, width)
    for at in range(0, width, step):
        cols = slice(at, at + step)
        x = jnp.concatenate([b[:, cols] for b in blocks], axis=0)
        y = lax.dot_general(pick, x, (((0,), (0,)), ((), ())), preferred_element_type=jnp.float32)
        y = y.astype(jnp.bfloat16)
        first = 0
        for out in (here, up1, down1, up2, down2):
            out[:, cols] = y[first : first + out.shape[0]]
            first += out.shape[0]


def dispatch(expert, blocks, width):
    rows = BLOCKS * ROWS

    def shape(n, w=width):
        return jax.ShapeDtypeStruct((n, w), jnp.bfloat16)

    return pl.pallas_call(
        dispatch_kernel,
        out_shape=(
            shape(2 * SEG), shape(2 * SEG), shape(2 * SEG), shape(SEG), shape(SEG),
            shape(rows, SLOTS), shape(rows, SLOTS),
        ),
        compiler_params=pltpu.CompilerParams(vmem_limit_bytes=VMEM),
        cost_estimate=pl.CostEstimate(
            flops=2 * rows * SLOTS * (width + rows), bytes_accessed=4 * 2**20, transcendentals=0
        ),
        name="dispatch",
    )(expert, *blocks)


def expert_kernel(core_ref, here, below, above, first2, second2, g0, u0, d0, g1, u1, d1,
                  here_o, below_o, above_o, first2_o, second2_o, x, acc):
    i = pl.program_id(0)
    turn, tile = i // TILES, i % TILES
    which = jnp.where(turn == 0, core_ref[0], 1 - core_ref[0])

    for e in range(2):
        @pl.when((tile == 0) & (which == e))
        def _():
            part = slice(e * SEG, (e + 1) * SEG)
            x[0:SEG] = here[part]
            x[SEG : 2 * SEG] = below[part]
            x[2 * SEG : 3 * SEG] = above[part]
            x[3 * SEG : 4 * SEG] = (first2, second2)[e][...]

    def work(g, u, d):
        gate = jnp.dot(x[...], g[0], preferred_element_type=jnp.float32)
        lift = jnp.dot(x[...], u[0], preferred_element_type=jnp.float32)
        hidden = (gate / (1.0 + jnp.exp(-gate)) * lift).astype(jnp.bfloat16)
        y = jnp.dot(hidden, d[0], preferred_element_type=jnp.float32)

        @pl.when(tile == 0)
        def _():
            acc[...] = y

        @pl.when(tile > 0)
        def _():
            acc[...] += y

    @pl.when(turn == 0)
    def _():
        work(g0, u0, d0)

    @pl.when(turn == 1)
    def _():
        work(g1, u1, d1)

    for e in range(2):
        @pl.when((tile == TILES - 1) & (which == e))
        def _():
            part = slice(e * SEG, (e + 1) * SEG)
            here_o[part] = acc[0:SEG].astype(jnp.bfloat16)
            below_o[part] = acc[SEG : 2 * SEG].astype(jnp.bfloat16)
            above_o[part] = acc[2 * SEG : 3 * SEG].astype(jnp.bfloat16)
            (first2_o, second2_o)[e][...] = acc[3 * SEG : 4 * SEG].astype(jnp.bfloat16)


def experts(core, pieces, own_gu, own_d, other_gu, other_d):
    width, hid = own_gu.shape[1], own_d.shape[1]
    tile = hid // TILES
    whole = [pl.BlockSpec(p.shape, lambda i, c: (0, 0)) for p in pieces]

    def early(i):
        return jnp.minimum(i, TILES - 1)

    def late(i):
        return jnp.maximum(i - TILES, 0)

    def weights(at):
        return [
            pl.BlockSpec((1, width, tile), lambda i, c: (0, 0, at(i))),
            pl.BlockSpec((1, width, tile), lambda i, c: (0, 0, at(i) + TILES)),
            pl.BlockSpec((1, tile, width), lambda i, c: (0, at(i), 0)),
        ]

    return pl.pallas_call(
        expert_kernel,
        grid_spec=pltpu.PrefetchScalarGridSpec(
            num_scalar_prefetch=1,
            grid=(2 * TILES,),
            in_specs=whole + weights(early) + weights(late),
            out_specs=whole,
            scratch_shapes=[
                pltpu.VMEM((4 * SEG, width), jnp.bfloat16),
                pltpu.VMEM((4 * SEG, width), jnp.float32),
            ],
        ),
        out_shape=[jax.ShapeDtypeStruct(p.shape, jnp.bfloat16) for p in pieces],
        compiler_params=pltpu.CompilerParams(vmem_limit_bytes=VMEM),
        cost_estimate=pl.CostEstimate(
            flops=2 * 8 * SEG * 3 * width * hid,
            bytes_accessed=2 * 3 * 2 * width * hid,
            transcendentals=8 * SEG * hid,
        ),
        name="experts",
    )(core, *pieces, own_gu, own_gu, own_d, other_gu, other_gu, other_d)


def combine_kernel(hi, lo, tokens, *refs):
    answers, outs = refs[:5], refs[5:]
    width = tokens.shape[1]
    step = min(512, width)
    for at in range(0, width, step):
        cols = slice(at, at + step)
        a = jnp.concatenate([r[:, cols] for r in answers], axis=0)
        y = jnp.dot(hi[...], a, preferred_element_type=jnp.float32)
        y = y + jnp.dot(lo[...], a, preferred_element_type=jnp.float32)
        outs[0][:, cols] = y[:ROWS] + tokens[:, cols].astype(jnp.float32)
        for b in range(1, BLOCKS):
            outs[b][:, cols] = y[b * ROWS : (b + 1) * ROWS].astype(jnp.bfloat16)


def combine(hi, lo, tokens, answers):
    shapes = [jax.ShapeDtypeStruct(tokens.shape, jnp.float32)]
    shapes += [jax.ShapeDtypeStruct(tokens.shape, jnp.bfloat16)] * (BLOCKS - 1)
    return pl.pallas_call(
        combine_kernel,
        out_shape=shapes,
        compiler_params=pltpu.CompilerParams(vmem_limit_bytes=VMEM),
        cost_estimate=pl.CostEstimate(
            flops=4 * BLOCKS * ROWS * SLOTS * tokens.shape[1], bytes_accessed=4 * 2**20, transcendentals=0
        ),
        name="combine",
    )(hi, lo, tokens, *answers)


def add(a, b):
    return (a.astype(jnp.float32) + b.astype(jnp.float32)).astype(jnp.bfloat16)


def body(tokens, norm_gain, route_ids, route_weight, gate_up, down):
    rows, ids, weights = tokens[0], route_ids[0], route_weight[0]
    width = rows.shape[1]
    count = lax.axis_size("expert")
    place = lax.axis_index("expert")
    chip, core = place // 2, place % 2

    other_gu = send(gate_up, 0, 0, other=True)
    other_d = send(down, 0, 0, other=True)

    values = rows.astype(jnp.float32)
    scale = lax.rsqrt(jnp.mean(values * values, axis=1, keepdims=True) + 1e-06)
    normed = (values * scale * norm_gain[None, :]).astype(jnp.bfloat16)
    share = weights / jnp.sum(weights, axis=1, keepdims=True)
    hi = lax.reduce_precision(share, 8, 7)
    lo = share - hi
    info = jnp.concatenate([ids.astype(jnp.float32), hi, lo], axis=1).astype(jnp.bfloat16)
    info = jnp.pad(info, ((0, 0), (0, INFO - info.shape[1])))
    p = [jnp.concatenate([normed, info], axis=1)]
    p.append(send(p[0], FAR, -FAR))
    q = [send(p[0], -FAR, FAR, other=True)]
    for _ in range(2):
        p.append(send(p[-1], FAR, -FAR))
        q.append(send(q[-1], FAR, -FAR))
    p.append(send(p[-1], FAR, -FAR))

    offsets = jnp.array([0, 1, 2, 3, -2, -1, 4, -3], jnp.int32)
    expert = (2 * chip + offsets) % count
    expert = jnp.broadcast_to(expert.astype(jnp.float32)[None, :, None], (8, 8, SEG)).reshape(8, SLOTS)
    here, up1, down1, up2, down2, hi, lo = dispatch(expert, p + q, width)
    below = send(up1, 1, 1)
    above = send(down1, -1, -1)
    first2 = send(up2, 2, 2)
    second2 = send(down2, -2, -2)
    here, below, above, first2, second2 = experts(
        core.reshape(1), [here, below, above, first2, second2], gate_up, down, other_gu, other_d
    )
    up1 = send(below, -1, -1)
    down1 = send(above, 1, 1)
    up2 = send(first2, -2, -2)
    down2 = send(second2, 2, 2)
    base, p1, p2, p3, p4, q1, q2, q3 = combine(hi, lo, rows, [here, up1, down1, up2, down2])
    base = send(base, 0, 0, onward=1)
    a = add(p3, send(p4, -FAR, FAR))
    b = add(q2, send(q3, -FAR, FAR))
    a = add(p2, send(a, -FAR, FAR))
    b = add(q1, send(b, -FAR, FAR))
    a = add(p1, send(a, -FAR, FAR))
    b = send(b, -FAR, FAR, other=True, onward=1)
    a = send(a, -FAR, FAR, onward=1)
    out = base + a.astype(jnp.float32) + b.astype(jnp.float32)
    return out.astype(jnp.bfloat16)[None]


def solution(mesh):
    placed = (
        P("section", "expert", None),
        P(),
        P("section", "expert", None),
        P("section", "expert", None),
        P("expert", None, None),
        P("expert", None, None),
    )
    return jax.shard_map(
        body, mesh=mesh, in_specs=placed, out_specs=P("section", "expert", None), check_vma=False
    )
```

```python
import functools

import jax
import jax.numpy as jnp
from jax import lax
from jax.experimental import pallas as pl
from jax.experimental.pallas import tpu as pltpu
from jax.sharding import PartitionSpec as P

CAP = 6
ROWS = 32
INFO = 128
FAR = 4
NEAR = FAR // 2
BLOCKS = 8
SEG = BLOCKS * CAP
SLOTS = 8 * SEG
TILES = 3


def send(value, up, down, other=False, onward=0):
    count, sections = lax.axis_size("expert"), lax.axis_size("section")

    def place(i):
        core = 1 - i % 2 if other else i % 2
        return ((i // 2 + (down if i % 2 else up)) * 2) % count + core

    if not onward:
        return lax.ppermute(value, "expert", [(i, place(i)) for i in range(count)])
    pairs = [
        (s * count + i, (s + onward) % sections * count + place(i))
        for s in range(sections)
        for i in range(count)
    ]
    return lax.ppermute(value, ("section", "expert"), pairs)


def prepare_kernel(tokens, gain, ids, weights, raw, ready):
    width = tokens.shape[2]
    values = tokens[0].astype(jnp.float32)
    scale = lax.rsqrt(jnp.mean(values * values, axis=1, keepdims=True) + 1e-06)
    share = weights[0] / jnp.sum(weights[0], axis=1, keepdims=True)
    hi = share.astype(jnp.bfloat16).astype(jnp.float32)
    lo = share - hi
    named = ids[0].astype(jnp.float32)
    lane = lax.broadcasted_iota(jnp.int32, (ROWS, INFO), 1)
    info = jnp.zeros((ROWS, INFO), jnp.float32)
    for k in range(8):
        info = jnp.where(lane == k, named[:, k : k + 1], info)
        info = jnp.where(lane == 8 + k, hi[:, k : k + 1], info)
        info = jnp.where(lane == 16 + k, lo[:, k : k + 1], info)
    info = info.astype(jnp.bfloat16)
    raw[:, :width] = tokens[0]
    raw[:, width:] = info
    ready[:, :width] = (values * scale * gain[...]).astype(jnp.bfloat16)
    ready[:, width:] = info


def prepare(tokens, gain, ids, weights):
    shape = jax.ShapeDtypeStruct((ROWS, tokens.shape[2] + INFO), jnp.bfloat16)
    return pl.pallas_call(
        prepare_kernel,
        out_shape=(shape, shape),
        compiler_params=pltpu.CompilerParams(vmem_limit_bytes=8 * 2**20),
        name="prepare",
    )(tokens, gain.reshape(1, -1), ids, weights)


def dispatch_kernel(count, place, raw, gain, *refs):
    blocks = refs[: BLOCKS - 1]
    *outs, hi_ref, lo_ref = refs[BLOCKS - 1 :]
    width = outs[0].shape[1]
    rows = BLOCKS * ROWS
    chip, core = place[0] >> 1, place[0] & 1
    info = jnp.concatenate([b[:, width:] for b in (raw, *blocks)], axis=0).astype(jnp.float32)
    group = lax.broadcasted_iota(jnp.int32, (1, SLOTS), 1) // SEG
    far = jnp.where(core == 0, 2 * NEAR, -2 * NEAR)
    offset = jnp.where(group < 4, group, jnp.where(group < 6, group - 6, group - 6 + far))
    expert = 2 * chip + offset
    expert = jnp.where(expert < 0, expert + count, expert)
    expert = jnp.where(expert >= count, expert - count, expert).astype(jnp.float32)
    member = jnp.zeros((rows, SLOTS), jnp.float32)
    hi = jnp.zeros((rows, SLOTS), jnp.float32)
    lo = jnp.zeros((rows, SLOTS), jnp.float32)
    for k in range(8):
        same = info[:, k : k + 1] == expert
        member = jnp.where(same, 1.0, member)
        hi = jnp.where(same, info[:, 8 + k : 9 + k], hi)
        lo = jnp.where(same, info[:, 16 + k : 17 + k], lo)
    r = lax.broadcasted_iota(jnp.int32, (rows, rows), 0)
    c = lax.broadcasted_iota(jnp.int32, (rows, rows), 1)
    before = jnp.where((c < r) & (c // ROWS == r // ROWS), 1.0, 0.0).astype(jnp.bfloat16)
    rank = jnp.dot(before, member.astype(jnp.bfloat16), preferred_element_type=jnp.float32)
    row_block = lax.broadcasted_iota(jnp.int32, (rows, SLOTS), 0) // ROWS
    q = lax.broadcasted_iota(jnp.int32, (1, SLOTS), 1) % SEG
    taken = (member > 0.5) & (rank == (q % CAP).astype(jnp.float32)) & (q // CAP == row_block)
    hi_ref[...] = jnp.where(taken, hi, 0.0).astype(jnp.bfloat16)
    lo_ref[...] = jnp.where(taken, lo, 0.0).astype(jnp.bfloat16)
    pick = jnp.where(taken, 1.0, 0.0).astype(jnp.bfloat16)
    values = raw[:, :width].astype(jnp.float32)
    scale = lax.rsqrt(jnp.mean(values * values, axis=1, keepdims=True) + 1e-06)
    step = min(512, width)
    for at in range(0, width, step):
        cols = slice(at, at + step)
        own = raw[:, cols].astype(jnp.float32) * scale * gain[:, cols]
        x = jnp.concatenate([own.astype(jnp.bfloat16)] + [b[:, cols] for b in blocks], axis=0)
        y = lax.dot_general(pick, x, (((0,), (0,)), ((), ())), preferred_element_type=jnp.float32)
        y = y.astype(jnp.bfloat16)
        for i, out in enumerate(outs):
            out[:, cols] = y[i * 2 * SEG : (i + 1) * 2 * SEG]


def dispatch(count, place, raw, gain, blocks):
    rows, width = BLOCKS * ROWS, raw.shape[1] - INFO
    vmem = pl.BlockSpec(memory_space=pltpu.VMEM)
    return pl.pallas_call(
        functools.partial(dispatch_kernel, count),
        in_specs=[pl.BlockSpec(memory_space=pltpu.SMEM)] + [vmem] * (BLOCKS + 1),
        out_shape=[jax.ShapeDtypeStruct((2 * SEG, width), jnp.bfloat16)] * 4
        + [jax.ShapeDtypeStruct((rows, SLOTS), jnp.bfloat16)] * 2,
        compiler_params=pltpu.CompilerParams(vmem_limit_bytes=24 * 2**20),
        cost_estimate=pl.CostEstimate(
            flops=2 * rows * SLOTS * (width + rows), bytes_accessed=4 * 2**20, transcendentals=0
        ),
        name="dispatch",
    )(place, raw, gain.reshape(1, -1), *blocks)


def expert_kernel(place, *refs):
    ins, (g0, u0, d0, g1, u1, d1), outs, (x, acc) = refs[:4], refs[4:10], refs[10:14], refs[14:]
    i = pl.program_id(0)
    turn, tile = i // TILES, i % TILES
    core = place[0] & 1
    which = jnp.where(turn == 0, core, 1 - core)

    for e in range(2):
        @pl.when((tile == 0) & (which == e))
        def _():
            for n, piece in enumerate(ins):
                x[n * SEG : (n + 1) * SEG] = piece[e * SEG : (e + 1) * SEG]

    def work(g, u, d):
        gate = jnp.dot(x[...], g[0], preferred_element_type=jnp.float32)
        lift = jnp.dot(x[...], u[0], preferred_element_type=jnp.float32)
        hidden = (gate / (1.0 + jnp.exp(-gate)) * lift).astype(jnp.bfloat16)
        y = jnp.dot(hidden, d[0], preferred_element_type=jnp.float32)

        @pl.when(tile == 0)
        def _():
            acc[...] = y

        @pl.when(tile > 0)
        def _():
            acc[...] += y

    @pl.when(turn == 0)
    def _():
        work(g0, u0, d0)

    @pl.when(turn == 1)
    def _():
        work(g1, u1, d1)

    for e in range(2):
        @pl.when((tile == TILES - 1) & (which == e))
        def _():
            for n, piece in enumerate(outs):
                piece[e * SEG : (e + 1) * SEG] = acc[n * SEG : (n + 1) * SEG].astype(jnp.bfloat16)


def experts(place, pieces, own_gu, own_d, other_gu, other_d):
    width, hid = own_gu.shape[1], own_d.shape[1]
    tile = hid // TILES
    whole = [pl.BlockSpec(p.shape, lambda i, c: (0, 0)) for p in pieces]

    def early(i):
        return jnp.minimum(i, TILES - 1)

    def late(i):
        return jnp.maximum(i - TILES, 0)

    def weights(at):
        return [
            pl.BlockSpec((1, width, tile), lambda i, c: (0, 0, at(i))),
            pl.BlockSpec((1, width, tile), lambda i, c: (0, 0, at(i) + TILES)),
            pl.BlockSpec((1, tile, width), lambda i, c: (0, at(i), 0)),
        ]

    return pl.pallas_call(
        expert_kernel,
        grid_spec=pltpu.PrefetchScalarGridSpec(
            num_scalar_prefetch=1,
            grid=(2 * TILES,),
            in_specs=whole + weights(early) + weights(late),
            out_specs=whole,
            scratch_shapes=[
                pltpu.VMEM((4 * SEG, width), jnp.bfloat16),
                pltpu.VMEM((4 * SEG, width), jnp.float32),
            ],
        ),
        out_shape=[jax.ShapeDtypeStruct(p.shape, jnp.bfloat16) for p in pieces],
        compiler_params=pltpu.CompilerParams(vmem_limit_bytes=32 * 2**20),
        cost_estimate=pl.CostEstimate(
            flops=2 * 8 * SEG * 3 * width * hid,
            bytes_accessed=2 * 3 * 2 * width * hid,
            transcendentals=8 * SEG * hid,
        ),
        name="experts",
    )(place, *pieces, own_gu, own_gu, own_d, other_gu, other_gu, other_d)


def combine_kernel(hi, lo, raw, *refs):
    answers, outs = refs[:4], refs[4:]
    width = outs[0].shape[1]
    step = min(512, width)
    for at in range(0, width, step):
        cols = slice(at, at + step)
        a = jnp.concatenate([r[:, cols] for r in answers], axis=0)
        y = jnp.dot(hi[...], a, preferred_element_type=jnp.float32)
        y = y + jnp.dot(lo[...], a, preferred_element_type=jnp.float32)
        outs[0][:, cols] = y[:ROWS] + raw[:, cols].astype(jnp.float32)
        for b in range(1, BLOCKS):
            outs[b][:, cols] = y[b * ROWS : (b + 1) * ROWS].astype(jnp.bfloat16)


def combine(hi, lo, raw, answers):
    width = raw.shape[1] - INFO
    shapes = [jax.ShapeDtypeStruct((ROWS, width), jnp.float32)]
    shapes += [jax.ShapeDtypeStruct((ROWS, width), jnp.bfloat16)] * (BLOCKS - 1)
    return pl.pallas_call(
        combine_kernel,
        out_shape=shapes,
        compiler_params=pltpu.CompilerParams(vmem_limit_bytes=24 * 2**20),
        cost_estimate=pl.CostEstimate(
            flops=4 * BLOCKS * ROWS * SLOTS * width, bytes_accessed=4 * 2**20, transcendentals=0
        ),
        name="combine",
    )(hi, lo, raw, *answers)


def add(a, b):
    return (a.astype(jnp.float32) + b.astype(jnp.float32)).astype(jnp.bfloat16)


def body(tokens, norm_gain, route_ids, route_weight, gate_up, down):
    count = lax.axis_size("expert")
    place = lax.axis_index("expert").reshape(1)
    raw, ready = prepare(tokens, norm_gain, route_ids, route_weight)

    a = [send(ready, FAR, FAR, onward=1)]
    b = [send(ready, -FAR, -FAR, onward=1)]
    raw = send(raw, 0, 0, onward=1)
    gate_up, down, a[0], b[0] = lax.optimization_barrier((gate_up, down, a[0], b[0]))
    other_gu = send(gate_up, 0, 0, other=True)
    other_d = send(down, 0, 0, other=True)
    for _ in range(2):
        a.append(send(a[-1], FAR, FAR))
        b.append(send(b[-1], -FAR, -FAR))
    a.append(send(a[-1], FAR, FAR))

    here, up, low, far, hi, lo = dispatch(count, place, raw, norm_gain, a + b)
    far = send(far, NEAR, -NEAR)
    up = send(up, 1, 1)
    low = send(low, -1, -1)
    here, up, low, far = experts(place, [here, up, low, far], gate_up, down, other_gu, other_d)
    far = send(far, -NEAR, NEAR)
    up = send(up, -1, -1)
    low = send(low, 1, 1)
    base, a1, a2, a3, a4, b1, b2, b3 = combine(hi, lo, raw, [here, up, low, far])
    x = add(a3, send(a4, -FAR, -FAR))
    y = add(b2, send(b3, FAR, FAR))
    x = add(a2, send(x, -FAR, -FAR))
    y = add(b1, send(y, FAR, FAR))
    x = add(a1, send(x, -FAR, -FAR))
    y = send(y, FAR, FAR)
    x = send(x, -FAR, -FAR)
    out = base + x.astype(jnp.float32) + y.astype(jnp.float32)
    return out.astype(jnp.bfloat16)[None]


def solution(mesh):
    placed = (
        P("section", "expert", None),
        P(),
        P("section", "expert", None),
        P("section", "expert", None),
        P("expert", None, None),
        P("expert", None, None),
    )
    return jax.shard_map(
        body, mesh=mesh, in_specs=placed, out_specs=P("section", "expert", None), check_vma=False
    )
```

```python
import functools

import jax
import jax.numpy as jnp
from jax import lax
from jax.experimental import pallas as pl
from jax.experimental.pallas import tpu as pltpu
from jax.sharding import PartitionSpec as P

CAP = 6
ROWS = 32
INFO = 128
FAR = 4
NEAR = FAR // 2
BLOCKS = 8
SEG = BLOCKS * CAP
SLOTS = 8 * SEG
TILES = 3


def send(value, up, down, other=False, onward=0):
    count, sections = lax.axis_size("expert"), lax.axis_size("section")

    def place(i):
        core = 1 - i % 2 if other else i % 2
        return ((i // 2 + (down if i % 2 else up)) * 2) % count + core

    if not onward:
        return lax.ppermute(value, "expert", [(i, place(i)) for i in range(count)])
    pairs = [
        (s * count + i, (s + onward) % sections * count + place(i))
        for s in range(sections)
        for i in range(count)
    ]
    return lax.ppermute(value, ("section", "expert"), pairs)


def prepare_kernel(tokens, gain, ids, weights, ready):
    width = tokens.shape[2]
    values = tokens[0].astype(jnp.float32)
    scale = lax.rsqrt(jnp.mean(values * values, axis=1, keepdims=True) + 1e-06)
    share = weights[0] / jnp.sum(weights[0], axis=1, keepdims=True)
    hi = share.astype(jnp.bfloat16).astype(jnp.float32)
    lo = share - hi
    named = ids[0].astype(jnp.float32)
    lane = lax.broadcasted_iota(jnp.int32, (ROWS, INFO), 1)
    info = jnp.zeros((ROWS, INFO), jnp.float32)
    for k in range(8):
        info = jnp.where(lane == k, named[:, k : k + 1], info)
        info = jnp.where(lane == 8 + k, hi[:, k : k + 1], info)
        info = jnp.where(lane == 16 + k, lo[:, k : k + 1], info)
    info = info.astype(jnp.bfloat16)
    ready[:, :width] = (values * scale * gain[...]).astype(jnp.bfloat16)
    ready[:, width:] = info


def prepare(tokens, gain, ids, weights):
    shape = jax.ShapeDtypeStruct((ROWS, tokens.shape[2] + INFO), jnp.bfloat16)
    return pl.pallas_call(
        prepare_kernel,
        out_shape=shape,
        compiler_params=pltpu.CompilerParams(vmem_limit_bytes=56 * 2**20),
        name="prepare",
    )(tokens, gain.reshape(1, -1), ids, weights)


def dispatch_kernel(count, place, *refs):
    blocks = refs[:BLOCKS]
    *outs, hi_ref, lo_ref = refs[BLOCKS:]
    width = outs[0].shape[1]
    rows = BLOCKS * ROWS
    chip = place[0] >> 1
    info = jnp.concatenate([b[:, width:] for b in blocks], axis=0).astype(jnp.float32)
    group = lax.broadcasted_iota(jnp.int32, (1, SLOTS), 1) // SEG
    offset = jnp.where(group < 4, group, jnp.where(group < 6, group - 6, jnp.where(group == 6, 4, -3)))
    expert = 2 * chip + offset
    expert = jnp.where(expert < 0, expert + count, expert)
    expert = jnp.where(expert >= count, expert - count, expert).astype(jnp.float32)
    member = jnp.zeros((rows, SLOTS), jnp.float32)
    hi = jnp.zeros((rows, SLOTS), jnp.float32)
    lo = jnp.zeros((rows, SLOTS), jnp.float32)
    for k in range(8):
        same = info[:, k : k + 1] == expert
        member = jnp.where(same, 1.0, member)
        hi = jnp.where(same, info[:, 8 + k : 9 + k], hi)
        lo = jnp.where(same, info[:, 16 + k : 17 + k], lo)
    r = lax.broadcasted_iota(jnp.int32, (rows, rows), 0)
    c = lax.broadcasted_iota(jnp.int32, (rows, rows), 1)
    before = jnp.where((c < r) & (c // ROWS == r // ROWS), 1.0, 0.0).astype(jnp.bfloat16)
    rank = jnp.dot(before, member.astype(jnp.bfloat16), preferred_element_type=jnp.float32)
    row_block = lax.broadcasted_iota(jnp.int32, (rows, SLOTS), 0) // ROWS
    q = lax.broadcasted_iota(jnp.int32, (1, SLOTS), 1) % SEG
    taken = (member > 0.5) & (rank == (q % CAP).astype(jnp.float32)) & (q // CAP == row_block)
    hi_ref[...] = jnp.where(taken, hi, 0.0).astype(jnp.bfloat16)
    lo_ref[...] = jnp.where(taken, lo, 0.0).astype(jnp.bfloat16)
    pick = jnp.where(taken, 1.0, 0.0).astype(jnp.bfloat16)
    step = min(512, width)
    for at in range(0, width, step):
        cols = slice(at, at + step)
        x = jnp.concatenate([b[:, cols] for b in blocks], axis=0)
        y = lax.dot_general(pick, x, (((0,), (0,)), ((), ())), preferred_element_type=jnp.float32)
        y = y.astype(jnp.bfloat16)
        first = 0
        for out in outs:
            out[:, cols] = y[first : first + out.shape[0]]
            first += out.shape[0]


def dispatch(count, place, blocks):
    rows, width = BLOCKS * ROWS, blocks[0].shape[1] - INFO
    vmem = pl.BlockSpec(memory_space=pltpu.VMEM)
    shapes = [(n * SEG, width) for n in (2, 2, 2, 1, 1)] + [(rows, SLOTS)] * 2
    return pl.pallas_call(
        functools.partial(dispatch_kernel, count),
        in_specs=[pl.BlockSpec(memory_space=pltpu.SMEM)] + [vmem] * BLOCKS,
        out_shape=[jax.ShapeDtypeStruct(shape, jnp.bfloat16) for shape in shapes],
        compiler_params=pltpu.CompilerParams(vmem_limit_bytes=24 * 2**20),
        cost_estimate=pl.CostEstimate(
            flops=2 * rows * SLOTS * (width + rows), bytes_accessed=4 * 2**20, transcendentals=0
        ),
        name="dispatch",
    )(place, *blocks)


def expert_kernel(n, place, *refs):
    ins, (g0, u0, d0, g1, u1, d1) = refs[:n], refs[n : n + 6]
    outs, (x, acc) = refs[n + 6 : 2 * n + 6], refs[2 * n + 6 :]
    i = pl.program_id(0)
    turn, tile = i // TILES, i % TILES
    core = place[0] & 1
    which = jnp.where(turn == 0, core, 1 - core)

    def parts(pieces, e):
        found = [piece.at[e * SEG : (e + 1) * SEG] for piece in pieces if piece.shape[0] == 2 * SEG]
        single = [piece for piece in pieces if piece.shape[0] == SEG]
        return found + single[e : e + 1]

    for e in range(2):
        @pl.when((tile == 0) & (which == e))
        def _():
            for at, piece in enumerate(parts(ins, e)):
                x[at * SEG : (at + 1) * SEG] = piece[...]

    def work(g, u, d):
        gate = jnp.dot(x[...], g[0], preferred_element_type=jnp.float32)
        lift = jnp.dot(x[...], u[0], preferred_element_type=jnp.float32)
        hidden = (gate / (1.0 + jnp.exp(-gate)) * lift).astype(jnp.bfloat16)
        y = jnp.dot(hidden, d[0], preferred_element_type=jnp.float32)

        @pl.when(tile == 0)
        def _():
            acc[...] = y

        @pl.when(tile > 0)
        def _():
            acc[...] += y

    @pl.when(turn == 0)
    def _():
        work(g0, u0, d0)

    @pl.when(turn == 1)
    def _():
        work(g1, u1, d1)

    for e in range(2):
        @pl.when((tile == TILES - 1) & (which == e))
        def _():
            for at, piece in enumerate(parts(outs, e)):
                piece[...] = acc[at * SEG : (at + 1) * SEG].astype(jnp.bfloat16)


def experts(place, pieces, own_gu, own_d, other_gu, other_d):
    width, hid = own_gu.shape[1], own_d.shape[1]
    tile = hid // TILES
    rows = sum(p.shape[0] for p in pieces) // 2
    whole = [pl.BlockSpec(p.shape, lambda i, c: (0, 0)) for p in pieces]

    def early(i):
        return jnp.minimum(i, TILES - 1)

    def late(i):
        return jnp.maximum(i - TILES, 0)

    def weights(at):
        return [
            pl.BlockSpec((1, width, tile), lambda i, c: (0, 0, at(i))),
            pl.BlockSpec((1, width, tile), lambda i, c: (0, 0, at(i) + TILES)),
            pl.BlockSpec((1, tile, width), lambda i, c: (0, at(i), 0)),
        ]

    return pl.pallas_call(
        functools.partial(expert_kernel, len(pieces)),
        grid_spec=pltpu.PrefetchScalarGridSpec(
            num_scalar_prefetch=1,
            grid=(2 * TILES,),
            in_specs=whole + weights(early) + weights(late),
            out_specs=whole,
            scratch_shapes=[
                pltpu.VMEM((rows, width), jnp.bfloat16),
                pltpu.VMEM((rows, width), jnp.float32),
            ],
        ),
        out_shape=[jax.ShapeDtypeStruct(p.shape, jnp.bfloat16) for p in pieces],
        compiler_params=pltpu.CompilerParams(vmem_limit_bytes=32 * 2**20),
        cost_estimate=pl.CostEstimate(
            flops=2 * 2 * rows * 3 * width * hid,
            bytes_accessed=2 * 3 * 2 * width * hid,
            transcendentals=2 * rows * hid,
        ),
        name="experts",
    )(place, *pieces, own_gu, own_gu, own_d, other_gu, other_gu, other_d)


def combine_kernel(hi, lo, tokens, *refs):
    answers, outs = refs[:5], refs[5:]
    width = outs[0].shape[1]
    step = min(512, width)
    for at in range(0, width, step):
        cols = slice(at, at + step)
        a = jnp.concatenate([r[:, cols] for r in answers], axis=0)
        y = jnp.dot(hi[...], a, preferred_element_type=jnp.float32)
        y = y + jnp.dot(lo[...], a, preferred_element_type=jnp.float32)
        outs[0][:, cols] = y[:ROWS] + tokens[0, :, cols].astype(jnp.float32)
        for b in range(1, BLOCKS):
            outs[b][:, cols] = y[b * ROWS : (b + 1) * ROWS].astype(jnp.bfloat16)


def combine(hi, lo, tokens, answers):
    width = tokens.shape[2]
    shapes = [jax.ShapeDtypeStruct((ROWS, width), jnp.float32)]
    shapes += [jax.ShapeDtypeStruct((ROWS, width), jnp.bfloat16)] * (BLOCKS - 1)
    return pl.pallas_call(
        combine_kernel,
        out_shape=shapes,
        compiler_params=pltpu.CompilerParams(vmem_limit_bytes=24 * 2**20),
        cost_estimate=pl.CostEstimate(
            flops=4 * BLOCKS * ROWS * SLOTS * width, bytes_accessed=4 * 2**20, transcendentals=0
        ),
        name="combine",
    )(hi, lo, tokens, *answers)


def add(a, b):
    return (a.astype(jnp.float32) + b.astype(jnp.float32)).astype(jnp.bfloat16)


def body(tokens, norm_gain, route_ids, route_weight, gate_up, down):
    count = lax.axis_size("expert")
    place = lax.axis_index("expert").reshape(1)

    p = [prepare(tokens, norm_gain, route_ids, route_weight)]
    p.append(send(p[0], FAR, -FAR))
    q = [send(p[0], -FAR, FAR, other=True)]
    for _ in range(2):
        p.append(send(p[-1], FAR, -FAR))
        q.append(send(q[-1], FAR, -FAR))
    gate_up, down, _, _ = lax.optimization_barrier((gate_up, down, p[2], q[1]))
    other_gu = send(gate_up, 0, 0, other=True)
    other_d = send(down, 0, 0, other=True)
    p.append(send(p[-1], FAR, -FAR))

    here, up1, low1, up2, low2, hi, lo = dispatch(count, place, p + q)
    up2 = send(up2, 2, 2)
    up1 = send(up1, 1, 1)
    low1 = send(low1, -1, -1)
    low2 = send(low2, -2, -2)
    weights = (gate_up, down, other_gu, other_d)
    [here] = experts(place, [here], *weights)
    here, up1, low1, up2, low2 = lax.optimization_barrier((here, up1, low1, up2, low2))
    up1, low1, up2, low2 = experts(place, [up1, low1, up2, low2], *weights)
    up1 = send(up1, -1, -1)
    low1 = send(low1, 1, 1)
    up2 = send(up2, -2, -2)
    low2 = send(low2, 2, 2)
    base, p1, p2, p3, p4, q1, q2, q3 = combine(hi, lo, tokens, [here, up1, low1, up2, low2])
    base = send(base, 0, 0, onward=1)
    x = add(p3, send(p4, -FAR, FAR))
    y = add(q2, send(q3, -FAR, FAR))
    x = add(p2, send(x, -FAR, FAR))
    y = add(q1, send(y, -FAR, FAR))
    x = add(p1, send(x, -FAR, FAR))
    y = send(y, -FAR, FAR, other=True, onward=1)
    x = send(x, -FAR, FAR, onward=1)
    out = base + x.astype(jnp.float32) + y.astype(jnp.float32)
    return out.astype(jnp.bfloat16)[None]


def solution(mesh):
    placed = (
        P("section", "expert", None),
        P(),
        P("section", "expert", None),
        P("section", "expert", None),
        P("expert", None, None),
        P("expert", None, None),
    )
    return jax.shard_map(
        body, mesh=mesh, in_specs=placed, out_specs=P("section", "expert", None), check_vma=False
    )
```

```python
import functools

import jax
import jax.numpy as jnp
from jax import lax
from jax.experimental import pallas as pl
from jax.experimental.pallas import tpu as pltpu
from jax.sharding import PartitionSpec as P

CAP = 6
ROWS = 32
INFO = 128
FAR = 4
NEAR = FAR // 2
BLOCKS = 8
SEG = BLOCKS * CAP
SLOTS = 8 * SEG
TILES = 3


def send(value, up, down, other=False, onward=0):
    count, sections = lax.axis_size("expert"), lax.axis_size("section")

    def place(i):
        core = 1 - i % 2 if other else i % 2
        return ((i // 2 + (down if i % 2 else up)) * 2) % count + core

    if not onward:
        return lax.ppermute(value, "expert", [(i, place(i)) for i in range(count)])
    pairs = [
        (s * count + i, (s + onward) % sections * count + place(i))
        for s in range(sections)
        for i in range(count)
    ]
    return lax.ppermute(value, ("section", "expert"), pairs)


def prepare_kernel(tokens, gain, ids, weights, ready):
    width = tokens.shape[2]
    values = tokens[0].astype(jnp.float32)
    scale = lax.rsqrt(jnp.mean(values * values, axis=1, keepdims=True) + 1e-06)
    share = weights[0] / jnp.sum(weights[0], axis=0, keepdims=True)
    hi = share.astype(jnp.bfloat16).astype(jnp.float32)
    unused = jnp.zeros((INFO - 24, ROWS), jnp.float32)
    columns = jnp.concatenate([ids[0].astype(jnp.float32), hi, share - hi, unused], axis=0)
    r = lax.broadcasted_iota(jnp.int32, (INFO, INFO), 0)
    c = lax.broadcasted_iota(jnp.int32, (INFO, INFO), 1)
    same = jnp.where(r == c, 1.0, 0.0).astype(jnp.bfloat16)
    info = lax.dot_general(
        columns.astype(jnp.bfloat16), same, (((0,), (0,)), ((), ())), preferred_element_type=jnp.float32
    ).astype(jnp.bfloat16)
    ready[:, :width] = (values * scale * gain[...]).astype(jnp.bfloat16)
    ready[:, width:] = info


def prepare(tokens, gain, ids, weights):
    shape = jax.ShapeDtypeStruct((ROWS, tokens.shape[2] + INFO), jnp.bfloat16)
    return pl.pallas_call(
        prepare_kernel,
        out_shape=shape,
        compiler_params=pltpu.CompilerParams(vmem_limit_bytes=56 * 2**20),
        name="prepare",
    )(tokens, gain.reshape(1, -1), ids.transpose(0, 2, 1), weights.transpose(0, 2, 1))


def dispatch_kernel(count, place, *refs):
    blocks = refs[:BLOCKS]
    *outs, hi_ref, lo_ref = refs[BLOCKS:]
    width = outs[0].shape[1]
    rows = BLOCKS * ROWS
    chip = place[0] >> 1
    info = jnp.concatenate([b[:, width:] for b in blocks], axis=0).astype(jnp.float32)
    group = lax.broadcasted_iota(jnp.int32, (1, SLOTS), 1) // SEG
    offset = jnp.where(group < 4, group, jnp.where(group < 6, group - 6, jnp.where(group == 6, 4, -3)))
    expert = 2 * chip + offset
    expert = jnp.where(expert < 0, expert + count, expert)
    expert = jnp.where(expert >= count, expert - count, expert).astype(jnp.float32)
    member = jnp.zeros((rows, SLOTS), jnp.float32)
    hi = jnp.zeros((rows, SLOTS), jnp.float32)
    lo = jnp.zeros((rows, SLOTS), jnp.float32)
    for k in range(8):
        same = info[:, k : k + 1] == expert
        member = jnp.where(same, 1.0, member)
        hi = jnp.where(same, info[:, 8 + k : 9 + k], hi)
        lo = jnp.where(same, info[:, 16 + k : 17 + k], lo)
    r = lax.broadcasted_iota(jnp.int32, (rows, rows), 0)
    c = lax.broadcasted_iota(jnp.int32, (rows, rows), 1)
    before = jnp.where((c < r) & (c // ROWS == r // ROWS), 1.0, 0.0).astype(jnp.bfloat16)
    rank = jnp.dot(before, member.astype(jnp.bfloat16), preferred_element_type=jnp.float32)
    row_block = lax.broadcasted_iota(jnp.int32, (rows, SLOTS), 0) // ROWS
    q = lax.broadcasted_iota(jnp.int32, (1, SLOTS), 1) % SEG
    taken = (member > 0.5) & (rank == (q % CAP).astype(jnp.float32)) & (q // CAP == row_block)
    hi_ref[...] = jnp.where(taken, hi, 0.0).astype(jnp.bfloat16)
    lo_ref[...] = jnp.where(taken, lo, 0.0).astype(jnp.bfloat16)
    pick = jnp.where(taken, 1.0, 0.0).astype(jnp.bfloat16)
    step = min(512, width)
    for at in range(0, width, step):
        cols = slice(at, at + step)
        x = jnp.concatenate([b[:, cols] for b in blocks], axis=0)
        y = lax.dot_general(pick, x, (((0,), (0,)), ((), ())), preferred_element_type=jnp.float32)
        y = y.astype(jnp.bfloat16)
        first = 0
        for out in outs:
            out[:, cols] = y[first : first + out.shape[0]]
            first += out.shape[0]


def dispatch(count, place, blocks):
    rows, width = BLOCKS * ROWS, blocks[0].shape[1] - INFO
    vmem = pl.BlockSpec(memory_space=pltpu.VMEM)
    shapes = [(n * SEG, width) for n in (2, 2, 2, 1, 1)] + [(rows, SLOTS)] * 2
    return pl.pallas_call(
        functools.partial(dispatch_kernel, count),
        in_specs=[pl.BlockSpec(memory_space=pltpu.SMEM)] + [vmem] * BLOCKS,
        out_shape=[jax.ShapeDtypeStruct(shape, jnp.bfloat16) for shape in shapes],
        compiler_params=pltpu.CompilerParams(vmem_limit_bytes=24 * 2**20),
        cost_estimate=pl.CostEstimate(
            flops=2 * rows * SLOTS * (width + rows), bytes_accessed=4 * 2**20, transcendentals=0
        ),
        name="dispatch",
    )(place, *blocks)


def expert_kernel(n, place, *refs):
    ins, (g0, u0, d0, g1, u1, d1) = refs[:n], refs[n : n + 6]
    outs, (x, acc) = refs[n + 6 : 2 * n + 6], refs[2 * n + 6 :]
    i = pl.program_id(0)
    turn, tile = i // TILES, i % TILES
    core = place[0] & 1
    which = jnp.where(turn == 0, core, 1 - core)

    def parts(pieces, e):
        found = [piece.at[e * SEG : (e + 1) * SEG] for piece in pieces if piece.shape[0] == 2 * SEG]
        single = [piece for piece in pieces if piece.shape[0] == SEG]
        return found + single[e : e + 1]

    for e in range(2):
        @pl.when((tile == 0) & (which == e))
        def _():
            for at, piece in enumerate(parts(ins, e)):
                x[at * SEG : (at + 1) * SEG] = piece[...]

    def work(g, u, d):
        gate = jnp.dot(x[...], g[0], preferred_element_type=jnp.float32)
        lift = jnp.dot(x[...], u[0], preferred_element_type=jnp.float32)
        hidden = (gate / (1.0 + jnp.exp(-gate)) * lift).astype(jnp.bfloat16)
        y = jnp.dot(hidden, d[0], preferred_element_type=jnp.float32)

        @pl.when(tile == 0)
        def _():
            acc[...] = y

        @pl.when(tile > 0)
        def _():
            acc[...] += y

    @pl.when(turn == 0)
    def _():
        work(g0, u0, d0)

    @pl.when(turn == 1)
    def _():
        work(g1, u1, d1)

    for e in range(2):
        @pl.when((tile == TILES - 1) & (which == e))
        def _():
            for at, piece in enumerate(parts(outs, e)):
                piece[...] = acc[at * SEG : (at + 1) * SEG].astype(jnp.bfloat16)


def experts(place, pieces, own_gu, own_d, other_gu, other_d):
    width, hid = own_gu.shape[1], own_d.shape[1]
    tile = hid // TILES
    rows = sum(p.shape[0] for p in pieces) // 2
    whole = [pl.BlockSpec(p.shape, lambda i, c: (0, 0)) for p in pieces]

    def early(i):
        return jnp.minimum(i, TILES - 1)

    def late(i):
        return jnp.maximum(i - TILES, 0)

    def weights(at):
        return [
            pl.BlockSpec((1, width, tile), lambda i, c: (0, 0, at(i))),
            pl.BlockSpec((1, width, tile), lambda i, c: (0, 0, at(i) + TILES)),
            pl.BlockSpec((1, tile, width), lambda i, c: (0, at(i), 0)),
        ]

    return pl.pallas_call(
        functools.partial(expert_kernel, len(pieces)),
        grid_spec=pltpu.PrefetchScalarGridSpec(
            num_scalar_prefetch=1,
            grid=(2 * TILES,),
            in_specs=whole + weights(early) + weights(late),
            out_specs=whole,
            scratch_shapes=[
                pltpu.VMEM((rows, width), jnp.bfloat16),
                pltpu.VMEM((rows, width), jnp.float32),
            ],
        ),
        out_shape=[jax.ShapeDtypeStruct(p.shape, jnp.bfloat16) for p in pieces],
        compiler_params=pltpu.CompilerParams(vmem_limit_bytes=56 * 2**20),
        cost_estimate=pl.CostEstimate(
            flops=2 * 2 * rows * 3 * width * hid,
            bytes_accessed=2 * 3 * 2 * width * hid,
            transcendentals=2 * rows * hid,
        ),
        name="experts",
    )(place, *pieces, own_gu, own_gu, own_d, other_gu, other_gu, other_d)


def combine_kernel(hi, lo, tokens, *refs):
    answers, outs = refs[:5], refs[5:]
    width = outs[0].shape[1]
    step = min(512, width)
    for at in range(0, width, step):
        cols = slice(at, at + step)
        a = jnp.concatenate([r[:, cols] for r in answers], axis=0)
        y = jnp.dot(hi[...], a, preferred_element_type=jnp.float32)
        y = y + jnp.dot(lo[...], a, preferred_element_type=jnp.float32)
        outs[0][:, cols] = y[:ROWS] + tokens[0, :, cols].astype(jnp.float32)
        for b in range(1, BLOCKS):
            outs[b][:, cols] = y[b * ROWS : (b + 1) * ROWS].astype(jnp.bfloat16)


def combine(hi, lo, tokens, answers):
    width = tokens.shape[2]
    shapes = [jax.ShapeDtypeStruct((ROWS, width), jnp.float32)]
    shapes += [jax.ShapeDtypeStruct((ROWS, width), jnp.bfloat16)] * (BLOCKS - 1)
    return pl.pallas_call(
        combine_kernel,
        out_shape=shapes,
        compiler_params=pltpu.CompilerParams(vmem_limit_bytes=24 * 2**20),
        cost_estimate=pl.CostEstimate(
            flops=4 * BLOCKS * ROWS * SLOTS * width, bytes_accessed=4 * 2**20, transcendentals=0
        ),
        name="combine",
    )(hi, lo, tokens, *answers)


def add(a, b):
    return (a.astype(jnp.float32) + b.astype(jnp.float32)).astype(jnp.bfloat16)


def body(tokens, norm_gain, route_ids, route_weight, gate_up, down):
    count = lax.axis_size("expert")
    place = lax.axis_index("expert").reshape(1)

    p = [prepare(tokens, norm_gain, route_ids, route_weight)]
    q = [send(p[0], 0, 0, other=True)]
    p.append(send(p[0], FAR, -FAR))
    other_gu = send(gate_up, 0, 0, other=True)
    other_d = send(down, 0, 0, other=True)
    for _ in range(3):
        q.append(send(q[-1], FAR, -FAR))
        p.append(send(p[-1], FAR, -FAR))

    here, up1, low1, up2, low2, hi, lo = dispatch(count, place, p + q[1:])
    up2 = send(up2, 2, 2)
    up1 = send(up1, 1, 1)
    low1 = send(low1, -1, -1)
    low2 = send(low2, -2, -2)
    weights = (gate_up, down, other_gu, other_d)
    [here] = experts(place, [here], *weights)
    here, up1, low1, up2, low2 = lax.optimization_barrier((here, up1, low1, up2, low2))
    up1, low1, up2, low2 = experts(place, [up1, low1, up2, low2], *weights)
    up1 = send(up1, -1, -1)
    low1 = send(low1, 1, 1)
    up2 = send(up2, -2, -2)
    low2 = send(low2, 2, 2)
    base, p1, p2, p3, p4, q1, q2, q3 = combine(hi, lo, tokens, [here, up1, low1, up2, low2])
    base = send(base, 0, 0, onward=1)
    x = add(p3, send(p4, -FAR, FAR))
    y = add(q2, send(q3, -FAR, FAR))
    x = add(p2, send(x, -FAR, FAR))
    y = add(q1, send(y, -FAR, FAR))
    x = add(p1, send(x, -FAR, FAR))
    y = send(y, -FAR, FAR, other=True, onward=1)
    x = send(x, -FAR, FAR, onward=1)
    out = base + x.astype(jnp.float32) + y.astype(jnp.float32)
    return out.astype(jnp.bfloat16)[None]


def solution(mesh):
    placed = (
        P("section", "expert", None),
        P(),
        P("section", "expert", None),
        P("section", "expert", None),
        P("expert", None, None),
        P("expert", None, None),
    )
    return jax.shard_map(
        body, mesh=mesh, in_specs=placed, out_specs=P("section", "expert", None), check_vma=False
    )
```

```python
import functools

import jax
import jax.numpy as jnp
from jax import lax
from jax.experimental import pallas as pl
from jax.experimental.pallas import tpu as pltpu
from jax.sharding import PartitionSpec as P

CAP = 6
ROWS = 32
INFO = 128
FAR = 4
NEAR = FAR // 2
BLOCKS = 8
SEG = BLOCKS * CAP
SLOTS = 8 * SEG
UP, TILES = 4, 3


def send(value, up, down, other=False, onward=0):
    count, sections = lax.axis_size("expert"), lax.axis_size("section")

    def place(i):
        core = 1 - i % 2 if other else i % 2
        return ((i // 2 + (down if i % 2 else up)) * 2) % count + core

    if not onward:
        return lax.ppermute(value, "expert", [(i, place(i)) for i in range(count)])
    pairs = [
        (s * count + i, (s + onward) % sections * count + place(i))
        for s in range(sections)
        for i in range(count)
    ]
    return lax.ppermute(value, ("section", "expert"), pairs)


def prepare_kernel(tokens, gain, ids, weights, ready):
    width = tokens.shape[2]
    values = tokens[0].astype(jnp.float32)
    scale = lax.rsqrt(jnp.mean(values * values, axis=1, keepdims=True) + 1e-06)
    share = weights[0] / jnp.sum(weights[0], axis=0, keepdims=True)
    hi = share.astype(jnp.bfloat16).astype(jnp.float32)
    unused = jnp.zeros((INFO - 24, ROWS), jnp.float32)
    columns = jnp.concatenate([ids[0].astype(jnp.float32), hi, share - hi, unused], axis=0)
    r = lax.broadcasted_iota(jnp.int32, (INFO, INFO), 0)
    c = lax.broadcasted_iota(jnp.int32, (INFO, INFO), 1)
    same = jnp.where(r == c, 1.0, 0.0).astype(jnp.bfloat16)
    info = lax.dot_general(
        columns.astype(jnp.bfloat16), same, (((0,), (0,)), ((), ())), preferred_element_type=jnp.float32
    ).astype(jnp.bfloat16)
    ready[:, :width] = (values * scale * gain[...]).astype(jnp.bfloat16)
    ready[:, width:] = info


def prepare(tokens, gain, ids, weights):
    shape = jax.ShapeDtypeStruct((ROWS, tokens.shape[2] + INFO), jnp.bfloat16)
    return pl.pallas_call(
        prepare_kernel,
        out_shape=shape,
        compiler_params=pltpu.CompilerParams(vmem_limit_bytes=56 * 2**20),
        name="prepare",
    )(tokens, gain.reshape(1, -1), ids.transpose(0, 2, 1), weights.transpose(0, 2, 1))


def dispatch_kernel(count, place, *refs):
    blocks = refs[:BLOCKS]
    *outs, hi_ref, lo_ref = refs[BLOCKS:]
    width = outs[0].shape[1]
    rows = BLOCKS * ROWS
    chip = place[0] >> 1
    info = jnp.concatenate([b[:, width:] for b in blocks], axis=0).astype(jnp.float32)
    group = lax.broadcasted_iota(jnp.int32, (1, SLOTS), 1) // SEG
    offset = jnp.where(group < 4, group, jnp.where(group < 6, group - 6, jnp.where(group == 6, 4, -3)))
    expert = 2 * chip + offset
    expert = jnp.where(expert < 0, expert + count, expert)
    expert = jnp.where(expert >= count, expert - count, expert).astype(jnp.float32)
    member = jnp.zeros((rows, SLOTS), jnp.float32)
    hi = jnp.zeros((rows, SLOTS), jnp.float32)
    lo = jnp.zeros((rows, SLOTS), jnp.float32)
    for k in range(8):
        same = info[:, k : k + 1] == expert
        member = jnp.where(same, 1.0, member)
        hi = jnp.where(same, info[:, 8 + k : 9 + k], hi)
        lo = jnp.where(same, info[:, 16 + k : 17 + k], lo)
    r = lax.broadcasted_iota(jnp.int32, (rows, rows), 0)
    c = lax.broadcasted_iota(jnp.int32, (rows, rows), 1)
    before = jnp.where((c < r) & (c // ROWS == r // ROWS), 1.0, 0.0).astype(jnp.bfloat16)
    rank = jnp.dot(before, member.astype(jnp.bfloat16), preferred_element_type=jnp.float32)
    row_block = lax.broadcasted_iota(jnp.int32, (rows, SLOTS), 0) // ROWS
    q = lax.broadcasted_iota(jnp.int32, (1, SLOTS), 1) % SEG
    taken = (member > 0.5) & (rank == (q % CAP).astype(jnp.float32)) & (q // CAP == row_block)
    hi_ref[...] = jnp.where(taken, hi, 0.0).astype(jnp.bfloat16)
    lo_ref[...] = jnp.where(taken, lo, 0.0).astype(jnp.bfloat16)
    pick = jnp.where(taken, 1.0, 0.0).astype(jnp.bfloat16)
    step = min(512, width)
    for at in range(0, width, step):
        cols = slice(at, at + step)
        x = jnp.concatenate([b[:, cols] for b in blocks], axis=0)
        y = lax.dot_general(pick, x, (((0,), (0,)), ((), ())), preferred_element_type=jnp.float32)
        y = y.astype(jnp.bfloat16)
        first = 0
        for out in outs:
            out[:, cols] = y[first : first + out.shape[0]]
            first += out.shape[0]


def dispatch(count, place, blocks):
    rows, width = BLOCKS * ROWS, blocks[0].shape[1] - INFO
    vmem = pl.BlockSpec(memory_space=pltpu.VMEM)
    shapes = [(n * SEG, width) for n in (2, 2, 2, 1, 1)] + [(rows, SLOTS)] * 2
    return pl.pallas_call(
        functools.partial(dispatch_kernel, count),
        in_specs=[pl.BlockSpec(memory_space=pltpu.SMEM)] + [vmem] * BLOCKS,
        out_shape=[jax.ShapeDtypeStruct(shape, jnp.bfloat16) for shape in shapes],
        compiler_params=pltpu.CompilerParams(vmem_limit_bytes=24 * 2**20),
        cost_estimate=pl.CostEstimate(
            flops=2 * rows * SLOTS * (width + rows), bytes_accessed=4 * 2**20, transcendentals=0
        ),
        name="dispatch",
    )(place, *blocks)


def expert_kernel(n, place, *refs):
    ins, sources, outs = refs[:n], refs[n : n + 4], refs[n + 4 : 2 * n + 4]
    x, wide, deep, acc, sems = refs[2 * n + 4 :]
    core = place[0] & 1
    hid, width = deep.shape[1], deep.shape[2]

    def fetch(turn, tile):
        to, at = (wide, tile) if tile < UP else (deep, tile - UP)
        step = to.shape[1] // (UP if tile < UP else TILES)
        rows = slice(at * step, (at + 1) * step)
        source = sources[2 * turn + (tile >= UP)]
        return pltpu.make_async_copy(source.at[0, rows], to.at[turn, rows], sems.at[turn, tile])

    for turn in range(2):
        for tile in range(UP + TILES):
            fetch(turn, tile).start()

    def parts(pieces, e):
        found = [piece.at[e * SEG : (e + 1) * SEG] for piece in pieces if piece.shape[0] == 2 * SEG]
        single = [piece for piece in pieces if piece.shape[0] == SEG]
        return found + single[e : e + 1]

    for turn in range(2):
        which = core if turn == 0 else 1 - core
        for e in range(2):
            @pl.when(which == e)
            def _():
                for at, piece in enumerate(parts(ins, e)):
                    x[at * SEG : (at + 1) * SEG] = piece[...]

        step = width // UP
        gated = None
        for tile in range(UP):
            fetch(turn, tile).wait()
            rows = slice(tile * step, (tile + 1) * step)
            y = jnp.dot(x[:, rows], wide[turn, rows], preferred_element_type=jnp.float32)
            gated = y if gated is None else gated + y
        gate = gated[:, :hid]
        hidden = (gate / (1.0 + jnp.exp(-gate)) * gated[:, hid:]).astype(jnp.bfloat16)
        step = hid // TILES
        for tile in range(TILES):
            fetch(turn, UP + tile).wait()
            rows = slice(tile * step, (tile + 1) * step)
            y = jnp.dot(hidden[:, rows], deep[turn, rows], preferred_element_type=jnp.float32)
            if tile == 0:
                acc[...] = y
            else:
                acc[...] += y
        for e in range(2):
            @pl.when(which == e)
            def _():
                for at, piece in enumerate(parts(outs, e)):
                    piece[...] = acc[at * SEG : (at + 1) * SEG].astype(jnp.bfloat16)


def experts(place, pieces, own_gu, own_d, other_gu, other_d):
    width, hid = own_gu.shape[1], own_d.shape[1]
    rows = sum(p.shape[0] for p in pieces) // 2
    vmem = [pl.BlockSpec(memory_space=pltpu.VMEM)] * len(pieces)
    return pl.pallas_call(
        functools.partial(expert_kernel, len(pieces)),
        in_specs=[pl.BlockSpec(memory_space=pltpu.SMEM)] + vmem + [pl.BlockSpec(memory_space=pl.ANY)] * 4,
        out_specs=vmem,
        out_shape=[jax.ShapeDtypeStruct(p.shape, jnp.bfloat16) for p in pieces],
        scratch_shapes=[
            pltpu.VMEM((rows, width), jnp.bfloat16),
            pltpu.VMEM((2, width, 2 * hid), jnp.bfloat16),
            pltpu.VMEM((2, hid, width), jnp.bfloat16),
            pltpu.VMEM((rows, width), jnp.float32),
            pltpu.SemaphoreType.DMA((2, UP + TILES)),
        ],
        compiler_params=pltpu.CompilerParams(vmem_limit_bytes=56 * 2**20),
        cost_estimate=pl.CostEstimate(
            flops=2 * 2 * rows * 3 * width * hid,
            bytes_accessed=2 * 3 * 2 * width * hid,
            transcendentals=2 * rows * hid,
        ),
        name="experts",
    )(place, *pieces, own_gu, own_d, other_gu, other_d)


def combine_kernel(hi, lo, tokens, *refs):
    answers, outs = refs[:5], refs[5:]
    width = outs[0].shape[1]
    step = min(512, width)
    for at in range(0, width, step):
        cols = slice(at, at + step)
        a = jnp.concatenate([r[:, cols] for r in answers], axis=0)
        y = jnp.dot(hi[...], a, preferred_element_type=jnp.float32)
        y = y + jnp.dot(lo[...], a, preferred_element_type=jnp.float32)
        outs[0][:, cols] = y[:ROWS] + tokens[0, :, cols].astype(jnp.float32)
        for b in range(1, BLOCKS):
            outs[b][:, cols] = y[b * ROWS : (b + 1) * ROWS].astype(jnp.bfloat16)


def combine(hi, lo, tokens, answers):
    width = tokens.shape[2]
    shapes = [jax.ShapeDtypeStruct((ROWS, width), jnp.float32)]
    shapes += [jax.ShapeDtypeStruct((ROWS, width), jnp.bfloat16)] * (BLOCKS - 1)
    return pl.pallas_call(
        combine_kernel,
        out_shape=shapes,
        compiler_params=pltpu.CompilerParams(vmem_limit_bytes=24 * 2**20),
        cost_estimate=pl.CostEstimate(
            flops=4 * BLOCKS * ROWS * SLOTS * width, bytes_accessed=4 * 2**20, transcendentals=0
        ),
        name="combine",
    )(hi, lo, tokens, *answers)


def add(a, b):
    return (a.astype(jnp.float32) + b.astype(jnp.float32)).astype(jnp.bfloat16)


def body(tokens, norm_gain, route_ids, route_weight, gate_up, down):
    count = lax.axis_size("expert")
    place = lax.axis_index("expert").reshape(1)

    p = [prepare(tokens, norm_gain, route_ids, route_weight)]
    q = [send(p[0], 0, 0, other=True)]
    p.append(send(p[0], FAR, -FAR))
    other_gu = send(gate_up, 0, 0, other=True)
    other_d = send(down, 0, 0, other=True)
    for _ in range(3):
        q.append(send(q[-1], FAR, -FAR))
        p.append(send(p[-1], FAR, -FAR))

    here, up1, low1, up2, low2, hi, lo = dispatch(count, place, p + q[1:])
    up2 = send(up2, 2, 2)
    up1 = send(up1, 1, 1)
    low1 = send(low1, -1, -1)
    low2 = send(low2, -2, -2)
    weights = (gate_up, down, other_gu, other_d)
    [here] = experts(place, [here], *weights)
    here, up1, low1, up2, low2 = lax.optimization_barrier((here, up1, low1, up2, low2))
    up1, low1, up2, low2 = experts(place, [up1, low1, up2, low2], *weights)
    up1 = send(up1, -1, -1)
    low1 = send(low1, 1, 1)
    up2 = send(up2, -2, -2)
    low2 = send(low2, 2, 2)
    base, p1, p2, p3, p4, q1, q2, q3 = combine(hi, lo, tokens, [here, up1, low1, up2, low2])
    base = send(base, 0, 0, onward=1)
    x = add(p3, send(p4, -FAR, FAR))
    y = add(q2, send(q3, -FAR, FAR))
    x = add(p2, send(x, -FAR, FAR))
    y = add(q1, send(y, -FAR, FAR))
    x = add(p1, send(x, -FAR, FAR))
    y = send(y, -FAR, FAR, other=True, onward=1)
    x = send(x, -FAR, FAR, onward=1)
    out = base + x.astype(jnp.float32) + y.astype(jnp.float32)
    return out.astype(jnp.bfloat16)[None]


def solution(mesh):
    placed = (
        P("section", "expert", None),
        P(),
        P("section", "expert", None),
        P("section", "expert", None),
        P("expert", None, None),
        P("expert", None, None),
    )
    return jax.shard_map(
        body, mesh=mesh, in_specs=placed, out_specs=P("section", "expert", None), check_vma=False
    )
```

```python
import functools

import jax
import jax.numpy as jnp
from jax import lax
from jax.experimental import pallas as pl
from jax.experimental.pallas import tpu as pltpu
from jax.sharding import PartitionSpec as P

CAP = 6
ROWS = 32
INFO = 128
FAR = 4
NEAR = FAR // 2
BLOCKS = 8
SEG = BLOCKS * CAP
SLOTS = 8 * SEG
UP, TILES = 4, 3


def send(value, up, down, other=False, onward=0):
    count, sections = lax.axis_size("expert"), lax.axis_size("section")

    def place(i):
        core = 1 - i % 2 if other else i % 2
        return ((i // 2 + (down if i % 2 else up)) * 2) % count + core

    if not onward:
        return lax.ppermute(value, "expert", [(i, place(i)) for i in range(count)])
    pairs = [
        (s * count + i, (s + onward) % sections * count + place(i))
        for s in range(sections)
        for i in range(count)
    ]
    return lax.ppermute(value, ("section", "expert"), pairs)


def prepare_kernel(tokens, gain, ids, weights, ready):
    width = tokens.shape[2]
    values = tokens[0].astype(jnp.float32)
    scale = lax.rsqrt(jnp.mean(values * values, axis=1, keepdims=True) + 1e-06)
    share = weights[0] / jnp.sum(weights[0], axis=0, keepdims=True)
    hi = share.astype(jnp.bfloat16).astype(jnp.float32)
    unused = jnp.zeros((INFO - 24, ROWS), jnp.float32)
    columns = jnp.concatenate([ids[0].astype(jnp.float32), hi, share - hi, unused], axis=0)
    r = lax.broadcasted_iota(jnp.int32, (INFO, INFO), 0)
    c = lax.broadcasted_iota(jnp.int32, (INFO, INFO), 1)
    same = jnp.where(r == c, 1.0, 0.0).astype(jnp.bfloat16)
    info = lax.dot_general(
        columns.astype(jnp.bfloat16), same, (((0,), (0,)), ((), ())), preferred_element_type=jnp.float32
    ).astype(jnp.bfloat16)
    ready[:, :width] = (values * scale * gain[...]).astype(jnp.bfloat16)
    ready[:, width:] = info


def prepare(tokens, gain, ids, weights):
    shape = jax.ShapeDtypeStruct((ROWS, tokens.shape[2] + INFO), jnp.bfloat16)
    return pl.pallas_call(
        prepare_kernel,
        out_shape=shape,
        compiler_params=pltpu.CompilerParams(vmem_limit_bytes=56 * 2**20),
        name="prepare",
    )(tokens, gain.reshape(1, -1), ids.transpose(0, 2, 1), weights.transpose(0, 2, 1))


def dispatch_kernel(count, place, *refs):
    blocks = refs[:BLOCKS]
    *outs, hi_ref, lo_ref = refs[BLOCKS:]
    width = outs[0].shape[1]
    rows = BLOCKS * ROWS
    chip = place[0] >> 1
    info = jnp.concatenate([b[:, width:] for b in blocks], axis=0).astype(jnp.float32)
    group = lax.broadcasted_iota(jnp.int32, (1, SLOTS), 1) // SEG
    offset = jnp.where(group < 4, group, jnp.where(group < 6, group - 6, jnp.where(group == 6, 4, -3)))
    expert = 2 * chip + offset
    expert = jnp.where(expert < 0, expert + count, expert)
    expert = jnp.where(expert >= count, expert - count, expert).astype(jnp.float32)
    member = jnp.zeros((rows, SLOTS), jnp.float32)
    hi = jnp.zeros((rows, SLOTS), jnp.float32)
    lo = jnp.zeros((rows, SLOTS), jnp.float32)
    for k in range(8):
        same = info[:, k : k + 1] == expert
        member = jnp.where(same, 1.0, member)
        hi = jnp.where(same, info[:, 8 + k : 9 + k], hi)
        lo = jnp.where(same, info[:, 16 + k : 17 + k], lo)
    r = lax.broadcasted_iota(jnp.int32, (rows, rows), 0)
    c = lax.broadcasted_iota(jnp.int32, (rows, rows), 1)
    before = jnp.where((c < r) & (c // ROWS == r // ROWS), 1.0, 0.0).astype(jnp.bfloat16)
    rank = jnp.dot(before, member.astype(jnp.bfloat16), preferred_element_type=jnp.float32)
    row_block = lax.broadcasted_iota(jnp.int32, (rows, SLOTS), 0) // ROWS
    q = lax.broadcasted_iota(jnp.int32, (1, SLOTS), 1) % SEG
    taken = (member > 0.5) & (rank == (q % CAP).astype(jnp.float32)) & (q // CAP == row_block)
    hi_ref[...] = jnp.where(taken, hi, 0.0).astype(jnp.bfloat16)
    lo_ref[...] = jnp.where(taken, lo, 0.0).astype(jnp.bfloat16)
    pick = jnp.where(taken, 1.0, 0.0).astype(jnp.bfloat16)
    step = min(512, width)
    for at in range(0, width, step):
        cols = slice(at, at + step)
        x = jnp.concatenate([b[:, cols] for b in blocks], axis=0)
        y = lax.dot_general(pick, x, (((0,), (0,)), ((), ())), preferred_element_type=jnp.float32)
        y = y.astype(jnp.bfloat16)
        first = 0
        for out in outs:
            out[:, cols] = y[first : first + out.shape[0]]
            first += out.shape[0]


def dispatch(count, place, blocks):
    rows, width = BLOCKS * ROWS, blocks[0].shape[1] - INFO
    vmem = pl.BlockSpec(memory_space=pltpu.VMEM)
    shapes = [(n * SEG, width) for n in (2, 2, 2, 1, 1)] + [(rows, SLOTS)] * 2
    return pl.pallas_call(
        functools.partial(dispatch_kernel, count),
        in_specs=[pl.BlockSpec(memory_space=pltpu.SMEM)] + [vmem] * BLOCKS,
        out_shape=[jax.ShapeDtypeStruct(shape, jnp.bfloat16) for shape in shapes],
        compiler_params=pltpu.CompilerParams(vmem_limit_bytes=24 * 2**20),
        cost_estimate=pl.CostEstimate(
            flops=2 * rows * SLOTS * (width + rows), bytes_accessed=4 * 2**20, transcendentals=0
        ),
        name="dispatch",
    )(place, *blocks)


def expert_kernel(n, place, *refs):
    ins, sources, outs = refs[:n], refs[n : n + 4], refs[n + 4 : 2 * n + 4]
    x, wide, deep, acc, sems = refs[2 * n + 4 :]
    core = place[0] & 1
    hid, width = deep.shape[1], deep.shape[2]

    def fetch(turn, tile):
        to, at = (wide, tile) if tile < UP else (deep, tile - UP)
        step = to.shape[1] // (UP if tile < UP else TILES)
        rows = slice(at * step, (at + 1) * step)
        source = sources[2 * turn + (tile >= UP)]
        return pltpu.make_async_copy(source.at[0, rows], to.at[turn, rows], sems.at[turn, tile])

    for turn in range(2):
        for tile in range(UP + TILES):
            fetch(turn, tile).start()

    def parts(pieces, e):
        found = [piece.at[e * SEG : (e + 1) * SEG] for piece in pieces if piece.shape[0] == 2 * SEG]
        single = [piece for piece in pieces if piece.shape[0] == SEG]
        return found + single[e : e + 1]

    for turn in range(2):
        which = core if turn == 0 else 1 - core
        for e in range(2):
            @pl.when(which == e)
            def _():
                for at, piece in enumerate(parts(ins, e)):
                    x[at * SEG : (at + 1) * SEG] = piece[...]

        step = width // UP
        gated = None
        for tile in range(UP):
            fetch(turn, tile).wait()
            rows = slice(tile * step, (tile + 1) * step)
            y = jnp.dot(x[:, rows], wide[turn, rows], preferred_element_type=jnp.float32)
            gated = y if gated is None else gated + y
        gate = gated[:, :hid]
        hidden = (gate / (1.0 + jnp.exp(-gate)) * gated[:, hid:]).astype(jnp.bfloat16)
        step = hid // TILES
        for tile in range(TILES):
            fetch(turn, UP + tile).wait()
            rows = slice(tile * step, (tile + 1) * step)
            y = jnp.dot(hidden[:, rows], deep[turn, rows], preferred_element_type=jnp.float32)
            if tile == 0:
                acc[...] = y
            else:
                acc[...] += y
        for e in range(2):
            @pl.when(which == e)
            def _():
                for at, piece in enumerate(parts(outs, e)):
                    piece[...] = acc[at * SEG : (at + 1) * SEG].astype(jnp.bfloat16)


def experts(place, pieces, own_gu, own_d, other_gu, other_d):
    width, hid = own_gu.shape[1], own_d.shape[1]
    rows = sum(p.shape[0] for p in pieces) // 2
    vmem = [pl.BlockSpec(memory_space=pltpu.VMEM)] * len(pieces)
    return pl.pallas_call(
        functools.partial(expert_kernel, len(pieces)),
        in_specs=[pl.BlockSpec(memory_space=pltpu.SMEM)] + vmem + [pl.BlockSpec(memory_space=pl.ANY)] * 4,
        out_specs=vmem,
        out_shape=[jax.ShapeDtypeStruct(p.shape, jnp.bfloat16) for p in pieces],
        scratch_shapes=[
            pltpu.VMEM((rows, width), jnp.bfloat16),
            pltpu.VMEM((2, width, 2 * hid), jnp.bfloat16),
            pltpu.VMEM((2, hid, width), jnp.bfloat16),
            pltpu.VMEM((rows, width), jnp.float32),
            pltpu.SemaphoreType.DMA((2, UP + TILES)),
        ],
        compiler_params=pltpu.CompilerParams(vmem_limit_bytes=50 * 2**20),
        cost_estimate=pl.CostEstimate(
            flops=2 * 2 * rows * 3 * width * hid,
            bytes_accessed=2 * 3 * 2 * width * hid,
            transcendentals=2 * rows * hid,
        ),
        name="experts",
    )(place, *pieces, own_gu, own_d, other_gu, other_d)


def combine_kernel(hi, lo, tokens, *refs):
    answers, outs = refs[:5], refs[5:]
    width = outs[0].shape[1]
    step = min(512, width)
    for at in range(0, width, step):
        cols = slice(at, at + step)
        a = jnp.concatenate([r[:, cols] for r in answers], axis=0)
        y = jnp.dot(hi[...], a, preferred_element_type=jnp.float32)
        y = y + jnp.dot(lo[...], a, preferred_element_type=jnp.float32)
        outs[0][:, cols] = y[:ROWS] + tokens[0, :, cols].astype(jnp.float32)
        for b in range(1, BLOCKS):
            outs[b][:, cols] = y[b * ROWS : (b + 1) * ROWS].astype(jnp.bfloat16)


def combine(hi, lo, tokens, answers):
    width = tokens.shape[2]
    shapes = [jax.ShapeDtypeStruct((ROWS, width), jnp.float32)]
    shapes += [jax.ShapeDtypeStruct((ROWS, width), jnp.bfloat16)] * (BLOCKS - 1)
    return pl.pallas_call(
        combine_kernel,
        out_shape=shapes,
        compiler_params=pltpu.CompilerParams(vmem_limit_bytes=24 * 2**20),
        cost_estimate=pl.CostEstimate(
            flops=4 * BLOCKS * ROWS * SLOTS * width, bytes_accessed=4 * 2**20, transcendentals=0
        ),
        name="combine",
    )(hi, lo, tokens, *answers)


def add(a, b):
    return (a.astype(jnp.float32) + b.astype(jnp.float32)).astype(jnp.bfloat16)


def body(tokens, norm_gain, route_ids, route_weight, gate_up, down):
    count = lax.axis_size("expert")
    place = lax.axis_index("expert").reshape(1)

    p = [prepare(tokens, norm_gain, route_ids, route_weight)]
    q = [send(p[0], 0, 0, other=True)]
    p.append(send(p[0], FAR, -FAR))
    other_gu = send(gate_up, 0, 0, other=True)
    other_d = send(down, 0, 0, other=True)
    for _ in range(3):
        q.append(send(q[-1], FAR, -FAR))
        p.append(send(p[-1], FAR, -FAR))

    here, up1, low1, up2, low2, hi, lo = dispatch(count, place, p + q[1:])
    up2 = send(up2, 2, 2)
    up1 = send(up1, 1, 1)
    low1 = send(low1, -1, -1)
    low2 = send(low2, -2, -2)
    weights = (gate_up, down, other_gu, other_d)
    [here] = experts(place, [here], *weights)
    up1, low1, up2, low2 = experts(place, [up1, low1, up2, low2], *weights)
    up1 = send(up1, -1, -1)
    low1 = send(low1, 1, 1)
    up2 = send(up2, -2, -2)
    low2 = send(low2, 2, 2)
    base, p1, p2, p3, p4, q1, q2, q3 = combine(hi, lo, tokens, [here, up1, low1, up2, low2])
    base = send(base, 0, 0, onward=1)
    x = add(p3, send(p4, -FAR, FAR))
    y = add(q2, send(q3, -FAR, FAR))
    x = add(p2, send(x, -FAR, FAR))
    y = add(q1, send(y, -FAR, FAR))
    x = add(p1, send(x, -FAR, FAR))
    y = send(y, -FAR, FAR, other=True, onward=1)
    x = send(x, -FAR, FAR, onward=1)
    out = base + x.astype(jnp.float32) + y.astype(jnp.float32)
    return out.astype(jnp.bfloat16)[None]


def solution(mesh):
    placed = (
        P("section", "expert", None),
        P(),
        P("section", "expert", None),
        P("section", "expert", None),
        P("expert", None, None),
        P("expert", None, None),
    )
    return jax.shard_map(
        body, mesh=mesh, in_specs=placed, out_specs=P("section", "expert", None), check_vma=False
    )
```
